32 devices in a mesh: groups: 2 (over x), az: 16 (over z, y, core).
Axes of the slice: x: 2, y: 2, z: 4, core: 2. Of those that a mesh axis runs over, the one named last changes fastest.
Arguments:
- flow_state: float32 [10, 512, 32, 128], P('groups', 'az'), parts along dimension 0, may hold values from -6 to 6
- source_amp: float32 [4, 32, 128], P('groups'), parts along dimension 0, may hold values from -3 to 3
- interface_values: float32 [10, 512, 128], P('groups'), parts along dimension 0, may hold values from -6 to 6
- interface_rows: int32 [8], P('groups'), parts along dimension 0, may hold values from 0 to 31
- band_order: int32 [6], replicated, may hold values from 0 to 5, each once
- band_coef: float32 [6], replicated, may hold values from -1.2 to 1.2
- pylon_orders: int32 [4], replicated, may hold values from 1 to 255
- pylon_coef: float32 [4, 2], replicated, may hold values from -0.6 to 0.6
Outputs:
- new_state: float32 [10, 512, 32, 128], P('groups', 'az'), parts along dimension 0
The draws below stay inside these ranges and needn't reach their ends.
There are 2 independent parts, one for each index of `groups`. The reference program is written for one: setup_inputs(seed, part) draws one part's arguments, and reference() takes and returns one part's arrays. A program takes and returns all parts, laid end to end along the dimension named above; an argument that names none is the same for every part. Nothing has to cross between parts.
All inputs are finite; a program needn't handle non-finite values.
Results may differ from the reference program's by a relative error of at most 0.00007.
Values sent between devices are 32-bit elements; how exact they have to be, the bound alone decides.
A program may use at most 64 MiB of HBM per device.

```python
import math
import jax
import jax.numpy as jnp
from jax import lax

A = 512
R = 128
X = 32
NI = 4
NP = 4
BLADES = 22


def touch_ends(entries, stream_key, low, largest):
    index_at = [jax.random.randint(jax.random.fold_in(stream_key, axis), (), 0, length) for axis, length in enumerate(entries.shape)]
    main_axis = entries.shape.index(max(entries.shape))
    next_to = index_at[:main_axis] + [(index_at[main_axis] + 1) % entries.shape[main_axis]] + index_at[main_axis + 1:]
    return entries.at[tuple(index_at)].set(low).at[tuple(next_to)].set(largest)


def steps_of(rng, shape, cuts, smallest, largest):
    level = 1.0
    for axis_at, blocks in cuts:
        steps = jax.random.uniform(jax.random.fold_in(jax.random.fold_in(rng, 6), axis_at), (blocks,), jnp.float32, smallest / len(cuts), largest / len(cuts))
        level = level * jnp.repeat(jnp.exp(steps), shape[axis_at] // blocks).reshape((-1,) + (1,) * (len(shape) - 1 - axis_at))
    return level


def centred(key, extent, scale, bound, split=(), held_as=jnp.bfloat16):
    array = jax.random.normal(key, extent, jnp.float32) * scale
    if len(split) > 0:
        array = steps_of(key, extent, split, -0.22, 0.18) * array
    return jnp.clip(array, min=-bound, max=bound).astype(held_as)


def setup_inputs(seed: int = 0, part: int = 0) -> dict:
    key_list = jax.random.split(jax.random.key(seed), 9)
    part_splits = jax.random.split(jax.random.fold_in(key_list[8], part), 9)
    return {
        "flow_state": centred(part_splits[0], (5, A, X, R), 1.0, 6.0, ((1, 16),), jnp.float32),
        "source_amp": centred(part_splits[1], (2, X, R), 0.5, 3.0, (), jnp.float32),
        "interface_values": centred(part_splits[2], (5, A, R), 1.0, 6.0, (), jnp.float32),
        "interface_rows": touch_ends(jax.random.randint(part_splits[3], (NI,), 0, X), jax.random.fold_in(part_splits[3], 1), 0, X - 1).astype(jnp.int32),
        "band_order": jax.random.permutation(key_list[4], 6).astype(jnp.int32),
        "band_coef": centred(key_list[5], (6,), 0.3, 1.2, (), jnp.float32),
        "pylon_orders": touch_ends(jax.random.randint(key_list[6], (NP,), 1, A // 2), jax.random.fold_in(key_list[6], 1), 1, (A // 2) - 1).astype(jnp.int32),
        "pylon_coef": centred(key_list[7], (NP, 2), 0.15, 0.6, (), jnp.float32),
    }


mean_axial = 0.5
mean_swirl = 0.4
hub_radius = 80.0
time_step = 0.2


def angle_table(left_ints, right_ints, whole_len):
    product = (left_ints[:, None] * right_ints[None, :]) % whole_len
    return product.astype(jnp.float32) * (2.0 * math.pi / whole_len)


def swirl_profile(stations, pylon_orders, pylon_coef, whole_len):
    angles = angle_table(stations, pylon_orders, whole_len)
    terms = pylon_coef[None, :, 0] * jnp.cos(angles) + pylon_coef[None, :, 1] * jnp.sin(angles)
    return mean_swirl + jnp.sum(terms, axis=1)


def tone_source(stations, source_amp, whole_len):
    angles = angle_table(stations, jnp.full((1,), BLADES, jnp.int32), whole_len)[:, 0]
    return jnp.cos(angles)[:, None, None] * source_amp[0][None] + jnp.sin(angles)[:, None, None] * source_amp[1][None]


def radial_band(current, band_order, band_coef):
    offsets = jnp.where(band_order < 3, band_order - 3, band_order - 2).astype(jnp.int32)
    width = current.shape[3]
    padded = jnp.pad(current, ((0, 0), (0, 0), (0, 0), (3, 3)))
    accum = jnp.zeros_like(current)
    for offset_idx in range(6):
        start = (3 + offsets[offset_idx]).astype(jnp.int32)
        accum = accum + band_coef[offset_idx] * lax.dynamic_slice_in_dim(padded, start, width, 3)
    return accum


def residual_terms(current, theta_part, axial_part, radial_part, swirl_vals, radius, forcing):
    inv_r = 1.0 / radius
    swirl_over_r = swirl_vals[:, None, None] * inv_r
    convect = mean_axial * axial_part + swirl_over_r[None] * theta_part
    divergence = axial_part[1] + radial_part[2] + (current[2] + theta_part[3]) * inv_r
    equations = [
        -convect[0] - divergence,
        -convect[1] - axial_part[4],
        -convect[2] - radial_part[4] + 2.0 * swirl_over_r * current[3],
        -convect[3] - theta_part[4] * inv_r - swirl_over_r * current[2],
        -convect[4] - divergence + forcing,
    ]
    return jnp.stack(equations)


def azimuth_derivative(current):
    spectrum = jnp.fft.rfft(current, axis=1)
    orders = jnp.arange(A // 2 + 1)
    orders = jnp.where(orders == A // 2, 0, orders)
    result = jnp.fft.irfft(spectrum * (1j * orders)[None, :, None, None], n=A, axis=1)
    return result.astype(jnp.float32)


def reference(flow_state, source_amp, interface_values, interface_rows, band_order, band_coef, pylon_orders, pylon_coef):
    stations = jnp.arange(A, dtype=jnp.int32)
    swirl_vals = swirl_profile(stations, pylon_orders, pylon_coef, A)
    radius = hub_radius + jnp.arange(R, dtype=jnp.float32)
    forcing = tone_source(stations, source_amp, A)
    row_mask = jnp.any(interface_rows[:, None] == jnp.arange(X, dtype=jnp.int32)[None, :], axis=0)

    def impose(current):
        return jnp.where(row_mask[None, None, :, None], interface_values[:, :, None, :], current)

    def evaluate(current):
        theta_part = azimuth_derivative(current)
        padded = jnp.pad(current, ((0, 0), (0, 0), (1, 1), (0, 0)))
        axial_part = 0.5 * (padded[:, :, 2:] - padded[:, :, :-2])
        radial_part = radial_band(current, band_order, band_coef)
        return residual_terms(current, theta_part, axial_part, radial_part, swirl_vals, radius, forcing)

    midway = impose(flow_state + (0.5 * time_step) * evaluate(flow_state))
    return impose(flow_state + time_step * evaluate(midway))
```

```python
import functools
import math

import jax
import jax.numpy as jnp
import ml_dtypes
import numpy as np
from jax import lax
from jax.experimental import pallas as pl
from jax.experimental.pallas import tpu as pltpu
from jax.sharding import PartitionSpec as P

mean_axial = 0.5
mean_swirl = 0.4
hub_radius = 80.0
time_step = 0.2
blades = 22
lane = 128
MESH = pl.DeviceIdType.MESH


def derivative_matrix(whole_len):
    shift = np.arange(whole_len)
    orders = np.arange(1, whole_len // 2)
    angles = (np.outer(shift, orders) % whole_len) * (2.0 * np.pi / whole_len)
    column = -(2.0 / whole_len) * (np.sin(angles) @ orders.astype(np.float64))
    full = column[(shift[:, None] - shift[None, :]) % whole_len]
    high = full.astype(ml_dtypes.bfloat16)
    low = (full - high.astype(np.float64)).astype(ml_dtypes.bfloat16)
    return high, low


def split_terms(value):
    high = value.astype(jnp.bfloat16)
    low = (value - high.astype(jnp.float32)).astype(jnp.bfloat16)
    return high, low


def product(left, right):
    dot = functools.partial(jnp.dot, preferred_element_type=jnp.float32)
    return dot(left[0], right[0]) + (dot(left[0], right[1]) + dot(left[1], right[0]))


def kernel(
    n, rows, local, fields, axial_len,
    flow, amp, imposed, rows_smem, order_smem, coef_smem, pylon_smem, pcoef_smem, d_high, d_low,
    out,
    packed, state, halo_left, halo_right, theta, radial, mid, mid_left, mid_right,
    returned, landed, swirl_r, forcing, band,
    send1, recv1, hsend, hrecv, msend, mrecv, send2, recv2,
):
    me = lax.axis_index("az")
    whole = n * local
    wide = rows * lane
    chunk = 64
    chunks = whole // chunk
    last = pl.ds(wide - lane, lane)
    first = pl.ds(0, lane)

    barrier = pltpu.get_barrier_semaphore()

    def greet(step, carry):
        pl.semaphore_signal(barrier, inc=1, device_id={"az": lax.rem(me + step, n)}, device_id_type=MESH)
        return carry

    lax.fori_loop(1, n, greet, 0)

    def span(block, size=local):
        return pl.ds(pl.multiple_of(block * size, 8), size)

    def pack(dest, store):
        for f in range(fields):
            for r in range(rows):
                start = f * local * axial_len + dest * rows + r
                store(f, r, flow[pl.ds(start, local, stride=axial_len), :])

    def store_own(f, r, value):
        state[f, span(me), r * lane:(r + 1) * lane] = value

    pack(me, store_own)
    pl.semaphore_wait(barrier, n - 1)

    def out_copy(step):
        dest = lax.rem(me + step, n)
        return pltpu.make_async_remote_copy(
            src_ref=packed.at[step], dst_ref=state.at[:, span(me), :],
            send_sem=send1.at[step], recv_sem=recv1.at[step],
            device_id={"az": dest}, device_id_type=MESH)

    def in_copy(step):
        source = lax.rem(me - step + n, n)
        return pltpu.make_async_remote_copy(
            src_ref=packed.at[step], dst_ref=state.at[:, span(source), :],
            send_sem=send1.at[step], recv_sem=recv1.at[step],
            device_id={"az": source}, device_id_type=MESH)

    def send_step(step, carry):
        def store(f, r, value):
            packed[step, f, :, r * lane:(r + 1) * lane] = value

        pack(lax.rem(me + step, n), store)
        out_copy(step).start()
        return carry

    lax.fori_loop(1, n, send_step, 0)

    lanes = lax.broadcasted_iota(jnp.int32, (1, wide), 1)
    inv_r = 1.0 / (hub_radius + (lanes % lane).astype(jnp.float32))
    row_id = lanes // lane + me * rows
    mask = row_id == rows_smem[0]
    for i in range(1, rows_smem.shape[0]):
        mask = mask | (row_id == rows_smem[i])

    def amp_row(part):
        pieces = [amp[part, pl.ds(me * rows + r, 1), :] for r in range(rows)]
        return jnp.concatenate(pieces, axis=1)

    amp_cos, amp_sin = amp_row(0), amp_row(1)

    def tables(block, carry):
        stations = block * chunk + lax.broadcasted_iota(jnp.int32, (chunk, lane), 0)

        def angle(order):
            return ((stations * order) & (whole - 1)).astype(jnp.float32) * (2.0 * math.pi / whole)

        swirl = jnp.full((chunk, lane), mean_swirl, jnp.float32)
        for p in range(pylon_smem.shape[0]):
            theta_p = angle(pylon_smem[p])
            swirl = swirl + (pcoef_smem[p, 0] * jnp.cos(theta_p) + pcoef_smem[p, 1] * jnp.sin(theta_p))
        tone = angle(blades)
        tone_cos, tone_sin = jnp.cos(tone), jnp.sin(tone)
        at = span(block, chunk)
        for r in range(rows):
            cols = slice(r * lane, (r + 1) * lane)
            swirl_r[at, cols] = swirl * inv_r[:, cols]
            forcing[at, cols] = tone_cos * amp_cos[:, cols] + tone_sin * amp_sin[:, cols]
        return carry

    lax.fori_loop(0, chunks, tables, 0)

    above = lax.broadcasted_iota(jnp.int32, (wide, wide), 0)
    across = lax.broadcasted_iota(jnp.int32, (wide, wide), 1)
    same = (above // lane) == (across // lane)
    shift = jnp.where(same, above - across, 0)
    band_full = jnp.zeros((wide, wide), jnp.float32)
    for k in range(order_smem.shape[0]):
        code = order_smem[k]
        offset = jnp.where(code < 3, code - 3, code - 2)
        band_full = band_full + jnp.where(shift == offset, coef_smem[k], 0.0)
    band[0], band[1] = split_terms(band_full)

    @pl.when(me == 0)
    def _():
        halo_left[...] = jnp.zeros_like(halo_left)
        mid_left[...] = jnp.zeros_like(mid_left)

    @pl.when(me == n - 1)
    def _():
        halo_right[...] = jnp.zeros_like(halo_right)
        mid_right[...] = jnp.zeros_like(mid_right)

    def to_right(block, step):
        return pltpu.make_async_remote_copy(
            src_ref=state.at[:, span(block), last], dst_ref=halo_left.at[:, span(block), :],
            send_sem=hsend.at[0, step], recv_sem=hrecv.at[0, step],
            device_id={"az": lax.rem(me + 1, n)}, device_id_type=MESH)

    def to_left(block, step):
        return pltpu.make_async_remote_copy(
            src_ref=state.at[:, span(block), first], dst_ref=halo_right.at[:, span(block), :],
            send_sem=hsend.at[1, step], recv_sem=hrecv.at[1, step],
            device_id={"az": lax.rem(me - 1 + n, n)}, device_id_type=MESH)

    def forward(block, step):
        @pl.when(me < n - 1)
        def _():
            to_right(block, step).start()

        @pl.when(me > 0)
        def _():
            to_left(block, step).start()

    forward(me, 0)

    def receive(step, carry):
        in_copy(step).wait_recv()
        forward(lax.rem(me - step + n, n), step)
        return carry

    lax.fori_loop(1, n, receive, 0)

    def derivatives(current):
        matrix = (d_high[...], d_low[...])

        def one(f, carry):
            theta[f] = product(matrix, split_terms(current[f]))
            return carry

        lax.fori_loop(0, fields, one, 0)
        stencil = (band[0], band[1])
        radial[0] = product(split_terms(current[2]), stencil)
        radial[1] = product(split_terms(current[4]), stencil)

    derivatives(state)

    def halo_wait(step, carry):
        @pl.when(me > 0)
        def _():
            to_right(lax.rem(me - 1 - step + n, n), step).wait_recv()

        @pl.when(me < n - 1)
        def _():
            to_left(lax.rem(me + 1 - step + n, n), step).wait_recv()

        return carry

    lax.fori_loop(0, n, halo_wait, 0)

    def stepped(current, left, right, at, size, factor):
        c = [current[f, at, :] for f in range(fields)]
        axial = []
        for f in range(fields):
            lower, upper = left[f, at, :], right[f, at, :]
            if rows > 1:
                lower = jnp.concatenate([lower, c[f][:, :wide - lane]], axis=1)
                upper = jnp.concatenate([c[f][:, lane:], upper], axis=1)
            axial.append(0.5 * (upper - lower))
        t = [theta[f, at, :] for f in range(fields)]
        wr = swirl_r[at, :]
        conv = [mean_axial * axial[f] + wr * t[f] for f in range(fields)]
        div = axial[1] + radial[0, at, :] + (c[2] + t[3]) * inv_r
        slope = [
            -conv[0] - div,
            -conv[1] - axial[4],
            -conv[2] - radial[1, at, :] + 2.0 * wr * c[3],
            -conv[3] - t[4] * inv_r - wr * c[2],
            -conv[4] - div + forcing[at, :],
        ]
        result = []
        for f in range(fields):
            fixed = jnp.concatenate([imposed[f, at, :]] * rows, axis=1)
            result.append(jnp.where(mask, fixed, state[f, at, :] + factor * slope[f]))
        return result

    def mid_to_right(block):
        return pltpu.make_async_remote_copy(
            src_ref=mid.at[:, span(block, chunk), last], dst_ref=mid_left.at[:, span(block, chunk), :],
            send_sem=msend.at[0, block], recv_sem=mrecv.at[0, block],
            device_id={"az": lax.rem(me + 1, n)}, device_id_type=MESH)

    def mid_to_left(block):
        return pltpu.make_async_remote_copy(
            src_ref=mid.at[:, span(block, chunk), first], dst_ref=mid_right.at[:, span(block, chunk), :],
            send_sem=msend.at[1, block], recv_sem=mrecv.at[1, block],
            device_id={"az": lax.rem(me - 1 + n, n)}, device_id_type=MESH)

    def first_half(block, carry):
        at = span(block, chunk)
        values = stepped(state, halo_left, halo_right, at, chunk, 0.5 * time_step)
        for f in range(fields):
            mid[f, at, :] = values[f]

        @pl.when(me < n - 1)
        def _():
            mid_to_right(block).start()

        @pl.when(me > 0)
        def _():
            mid_to_left(block).start()

        return carry

    lax.fori_loop(0, chunks, first_half, 0)

    derivatives(mid)

    def mid_wait(block, carry):
        @pl.when(me > 0)
        def _():
            mid_to_right(block).wait_recv()

        @pl.when(me < n - 1)
        def _():
            mid_to_left(block).wait_recv()

        return carry

    lax.fori_loop(0, chunks, mid_wait, 0)

    def back_copy(step, other):
        return pltpu.make_async_remote_copy(
            src_ref=returned.at[step], dst_ref=landed.at[step],
            send_sem=send2.at[step], recv_sem=recv2.at[step],
            device_id={"az": other}, device_id_type=MESH)

    def second_half(step, carry):
        dest = lax.rem(me + step, n)
        values = stepped(mid, mid_left, mid_right, span(dest), local, time_step)
        for f in range(fields):
            returned[step, f] = values[f]
        back_copy(step, dest).start()
        return carry

    lax.fori_loop(1, n, second_half, 0)

    def unpack(source, f, r, value):
        start = f * local * axial_len + source * rows + r
        out[pl.ds(start, local, stride=axial_len), :] = value

    own = stepped(mid, mid_left, mid_right, span(me), local, time_step)
    for f in range(fields):
        for r in range(rows):
            unpack(me, f, r, own[f][:, r * lane:(r + 1) * lane])

    def collect(step, carry):
        source = lax.rem(me - step + n, n)
        back_copy(step, source).wait_recv()
        for f in range(fields):
            for r in range(rows):
                unpack(source, f, r, landed[step, f, :, r * lane:(r + 1) * lane])
        return carry

    lax.fori_loop(1, n, collect, 0)

    def drain(step, carry):
        out_copy(step).wait_send()
        back_copy(step, lax.rem(me + step, n)).wait_send()
        return carry

    lax.fori_loop(1, n, drain, 0)

    def drain_halo(step, carry):
        @pl.when(me < n - 1)
        def _():
            to_right(lax.rem(me - step + n, n), step).wait_send()

        @pl.when(me > 0)
        def _():
            to_left(lax.rem(me - step + n, n), step).wait_send()

        return carry

    lax.fori_loop(0, n, drain_halo, 0)

    def drain_mid(block, carry):
        @pl.when(me < n - 1)
        def _():
            mid_to_right(block).wait_send()

        @pl.when(me > 0)
        def _():
            mid_to_left(block).wait_send()

        return carry

    lax.fori_loop(0, chunks, drain_mid, 0)


def per_device(
    flow_state, source_amp, interface_values, interface_rows, band_order, band_coef, pylon_orders, pylon_coef
):
    n = lax.axis_size("az")
    fields, local, axial_len, radial_len = flow_state.shape
    rows = axial_len // n
    whole = local * n
    wide = rows * radial_len
    chunks = whole // 64
    high, low = derivative_matrix(whole)
    vmem = pl.BlockSpec(memory_space=pltpu.VMEM)
    smem = pl.BlockSpec(memory_space=pltpu.SMEM)
    flat = (fields * local * axial_len, radial_len)
    f32 = jnp.float32
    call = pl.pallas_call(
        functools.partial(kernel, n, rows, local, fields, axial_len),
        out_shape=jax.ShapeDtypeStruct(flat, f32),
        in_specs=[vmem, vmem, vmem, smem, smem, smem, smem, smem, vmem, vmem],
        out_specs=vmem,
        scratch_shapes=[
            pltpu.VMEM((n, fields, local, wide), f32),
            pltpu.VMEM((fields, whole, wide), f32),
            pltpu.VMEM((fields, whole, lane), f32),
            pltpu.VMEM((fields, whole, lane), f32),
            pltpu.VMEM((fields, whole, wide), f32),
            pltpu.VMEM((2, whole, wide), f32),
            pltpu.VMEM((fields, whole, wide), f32),
            pltpu.VMEM((fields, whole, lane), f32),
            pltpu.VMEM((fields, whole, lane), f32),
            pltpu.VMEM((n, fields, local, wide), f32),
            pltpu.VMEM((n, fields, local, wide), f32),
            pltpu.VMEM((whole, wide), f32),
            pltpu.VMEM((whole, wide), f32),
            pltpu.VMEM((2, wide, wide), jnp.bfloat16),
            pltpu.SemaphoreType.DMA((n,)),
            pltpu.SemaphoreType.DMA((n,)),
            pltpu.SemaphoreType.DMA((2, n)),
            pltpu.SemaphoreType.DMA((2, n)),
            pltpu.SemaphoreType.DMA((2, chunks)),
            pltpu.SemaphoreType.DMA((2, chunks)),
            pltpu.SemaphoreType.DMA((n,)),
            pltpu.SemaphoreType.DMA((n,)),
        ],
        compiler_params=pltpu.CompilerParams(
            collective_id=0, has_side_effects=True, vmem_limit_bytes=52 * 1024 * 1024
        ),
    )
    result = call(
        flow_state.reshape(flat), source_amp, interface_values, interface_rows, band_order, band_coef,
        pylon_orders, pylon_coef, jnp.asarray(high), jnp.asarray(low),
    )
    return result.reshape(flow_state.shape)


def solution(mesh):
    placed = (
        P("groups", "az", None, None),
        P("groups", None, None),
        P("groups", None, None),
        P("groups"),
        P(),
        P(),
        P(),
        P(),
    )
    return jax.shard_map(
        per_device, mesh=mesh, in_specs=placed, out_specs=P("groups", "az", None, None), check_vma=False
    )
```
